32 devices in a mesh: lat: 16 (over z, y, x), mem: 2 (over core).
Axes of the slice: x: 2, y: 2, z: 4, core: 2. Of those that a mesh axis runs over, the one named last changes fastest.
Arguments:
- obs_rows: float32 [16384, 32], P(('lat', 'mem')), may hold values from -0.18 to 0.18
- obs_band: int32 [16384, 1], P(('lat', 'mem')), may hold values from 0 to 15; in each aligned block of 512 rows (0 to 511, 512 to 1023, ...) at most 32 rows name the same one
- obs_cell: int32 [16384], P(('lat', 'mem')), may hold values from 0 to 1439
- obs_top: int32 [16384], P(('lat', 'mem')), may hold values from 1 to 32
- perturb: bfloat16 [16, 1440, 256], P('lat', None, 'mem'), may hold values from -6 to 6
- control: bfloat16 [16, 1440, 256], P('lat', None, 'mem'), may hold values from -6 to 6
Outputs:
- gradient: float32 [16, 1440, 256], P('lat', None, 'mem')
The draws below stay inside these ranges and needn't reach their ends.
Inputs may be any that keep to these rules, and one draw needn't show every extreme that they name: `obs_band`: the 512 profiles of one device name one band each; no band is named by more than 32 profiles of one device. `obs_cell`: row within the band times 1440 plus the longitude column. `obs_top`: levels below this index carry the profile; the rest are unused.
All inputs are finite; a program needn't handle non-finite values.
Results may differ from the reference program's by a relative error of at most 0.0003.
Values sent between devices are 32-bit elements; how exact they have to be, the bound alone decides.
A program may use at most 64 MiB of HBM per device.

```python
import math
import jax
import jax.numpy as jnp
import numpy as np
from jax import lax

LAT_DEV = 1
LON = 1440
LEV = 32
OBS_DEV = 512
CAP = 32
NLAT = 16
MEMBERS = 8
OBS = 16384
N_LAT = 16


def place_ends(result, stream_key, low, top_value):
    extent = result.shape
    place = [jax.random.randint(jax.random.fold_in(stream_key, axis), (), 0, extent[axis]) for axis in range(len(extent))]
    result = result.at[tuple(place)].set(low)
    longest = extent.index(max(extent))
    place[longest] = (place[longest] + 1) % extent[longest]
    return result.at[tuple(place)].set(top_value)


def levels(rng, dims, shards, smallest, top_value):
    level = 1.0
    for dim, parts in shards:
        draws = jax.random.uniform(jax.random.fold_in(jax.random.fold_in(rng, 6), dim), (parts,), jnp.float32, smallest / len(shards), top_value / len(shards))
        level = level * jnp.repeat(jnp.exp(draws), dims[dim] // parts).reshape((-1,) + (1,) * (len(dims) - 1 - dim))
    return level


def shared_out(rng, own, number, rows, count, top, limit, slope):
    order = jax.random.permutation(rng, count)
    heavy_load, ordinary = shares(count, rows * top, limit, slope, True), shares(count, rows * top, limit, slope, False)
    places = jnp.arange(count)

    def named(lengths, rotation):
        used = int((lengths > 0).sum())
        fixed = max(1, used // 4)
        passed = fixed + (places - fixed + rotation * (used - fixed)) % max(1, count - fixed)
        return jnp.zeros((count,), jnp.int32).at[order[jnp.where(places < fixed, places, passed)]].set(jnp.asarray(lengths, jnp.int32))

    lengths = jnp.where(number % 4 == 0, named(heavy_load, number // 4), named(ordinary, number - number // 4 - 1))
    mixed = jax.random.permutation(jax.random.fold_in(own, 3), count)
    source_of, sink = mixed[0:count // 2 * 2:2], mixed[1:count // 2 * 2:2]
    margin = jnp.minimum(lengths[source_of] - 1, limit - lengths[sink]) // 2
    margin = jnp.where((source_of == order[0]) | (sink == order[0]) | (lengths[sink] == 0), 0, jnp.maximum(margin, 0))
    passed = jax.random.randint(jax.random.fold_in(own, 4), (count // 2,), 0, 1 << 20) % (margin + 1)
    lengths = lengths.at[source_of].add(-passed).at[sink].add(passed)
    items = jnp.searchsorted(jnp.cumsum(lengths), jnp.arange(rows * top), side="right").astype(jnp.int32)
    listing = items.reshape(top, rows).T
    listing = listing[jax.random.permutation(jax.random.fold_in(own, 1), rows)]
    rotation = jax.random.randint(jax.random.fold_in(own, 2), (rows, 1), 0, top)
    return jnp.take_along_axis(listing, (jnp.arange(top)[None, :] + rotation) % top, axis=1)


def shares(amount, total, bound, slope, full):
    weights = [(1 << 20) // math.isqrt(standing ** slope) + 1 for standing in range(1, amount + 1)]
    largest = bound if full else min(bound, max(-(-total // amount), total * weights[0] // sum(weights)))
    least = 1 if total - largest >= amount - 1 else 0
    counts, spare = [largest] + [least] * (amount - 1), total - largest - least * (amount - 1)
    while spare > 0:
        movable = [i for i in range(1, amount) if counts[i] < largest] or [i for i in range(1, amount) if counts[i] < bound]
        pool, budget = sum([weights[i] for i in movable]), spare
        for i in movable:
            extra = min(bound - counts[i], max(1, budget * weights[i] // pool), spare)
            counts[i] = counts[i] + extra
            spare = spare - extra
    return np.array(counts)


def noise(rng, extent, width, limit, shards=(), held_as=jnp.bfloat16):
    result = width * jax.random.normal(rng, extent, jnp.float32)
    if shards:
        result = result * levels(rng, extent, shards, -0.22, 0.18)
    return jnp.clip(result, -limit, limit).astype(held_as)


def setup_inputs(seed: int = 0) -> dict:
    arg_keys = jax.random.split(jax.random.key(seed), 7)
    obs_rows = noise(arg_keys[0], (OBS, LEV), 0.03, 0.18, ((0, 32),), jnp.float32)
    obs_band_keys = jax.random.split(jax.random.fold_in(arg_keys[1], 1), OBS // OBS_DEV)
    obs_band_turns = jax.random.permutation(jax.random.fold_in(arg_keys[1], 3), OBS // OBS_DEV)
    obs_band = jax.vmap(lambda own, number: shared_out(jax.random.fold_in(arg_keys[1], 2), own, number, OBS_DEV, N_LAT, 1, CAP, 2))(obs_band_keys, obs_band_turns).reshape((OBS, 1))
    obs_cell = place_ends(jax.random.randint(arg_keys[2], (OBS,), 0, LAT_DEV * LON), jax.random.fold_in(arg_keys[2], 1), 0, (LAT_DEV * LON) - 1).astype(jnp.int32)
    obs_top = place_ends(jax.random.randint(arg_keys[3], (OBS,), 1, LEV + 1), jax.random.fold_in(arg_keys[3], 1), 1, LEV).astype(jnp.int32)
    perturb = noise(arg_keys[4], (NLAT, LON, MEMBERS * LEV), 1.0, 6.0, ((0, 16), (2, 2)))
    control = noise(arg_keys[5], (NLAT, LON, MEMBERS * LEV), 1.0, 6.0, ((0, 16), (2, 2)))
    return dict(obs_rows=obs_rows, obs_band=obs_band, obs_cell=obs_cell, obs_top=obs_top, perturb=perturb, control=control)


def kernel(count, spread, periodic):
    positions = jnp.arange(count, dtype=jnp.float32)
    distance = jnp.abs(positions[:, None] - positions[None, :])
    if periodic:
        distance = jnp.minimum(distance, count - distance)
    return jnp.exp(-0.5 * (distance / spread) ** 2)


def lon_spread(row, all_rows, lon_count):
    base = float(max(lon_count // 60, 4))
    latitude = 1.2 * (row.astype(jnp.float32) + 0.5) / all_rows
    return base / jnp.cos(latitude)


def reference(obs_rows, obs_band, obs_cell, obs_top, perturb, control):
    level_ids = jnp.arange(LEV, dtype=jnp.int32)
    level_mask = (level_ids[None, :] < obs_top[:, None]).astype(jnp.float32)
    profiles = obs_rows * level_mask
    flat_index = (obs_band[:, 0] * (LAT_DEV * LON) + obs_cell).astype(jnp.int32)
    innovation = jnp.zeros((NLAT * LON, LEV), jnp.float32).at[flat_index].add(profiles)
    innovation = innovation.reshape(NLAT, LON, LEV)
    vert = kernel(LEV, 1.0, False)
    latk = kernel(NLAT, 8.0 * LAT_DEV, False)
    members_view = perturb.reshape(NLAT, LON, MEMBERS, LEV)

    def member_field(member):
        slab = lax.dynamic_index_in_dim(members_view, member, 2, keepdims=False).astype(jnp.float32)
        product = slab * innovation
        vertical = jnp.einsum('ml,rjl->rjm', vert, product, precision=lax.Precision.HIGHEST)
        return jnp.einsum('rR,Rjm->rjm', latk, vertical, precision=lax.Precision.HIGHEST)

    fields = lax.map(member_field, jnp.arange(MEMBERS, dtype=jnp.int32))

    def row_field(row):
        lonk = kernel(LON, lon_spread(row, NLAT, LON), True)
        data = lax.dynamic_index_in_dim(fields, row, 1, keepdims=False)
        smoothed = jnp.einsum('jJ,kJl->jkl', lonk, data, precision=lax.Precision.HIGHEST)
        return smoothed.reshape(LON, MEMBERS * LEV)

    zonal = lax.map(row_field, jnp.arange(NLAT, dtype=jnp.int32))
    return control.astype(jnp.float32) + zonal
```

```python
import functools
import math

import jax
import jax.numpy as jnp
import numpy as np
from jax import lax
from jax.experimental import pallas as pl
from jax.experimental.pallas import tpu as pltpu
from jax.sharding import PartitionSpec as P

CAP = 32
PARTS = 3
BLOCKS = 3
QUADS = 4
HIGHEST = lax.Precision.HIGHEST
F32 = jnp.float32
BF16 = jnp.bfloat16


def iota(shape, axis):
    return lax.broadcasted_iota(jnp.int32, shape, axis)


def split(value):
    high = value.astype(BF16)
    return high, (value - high.astype(F32)).astype(BF16)


def dot(left, right):
    return jnp.dot(left, right, preferred_element_type=F32)


def make_messages(me, meta_ref, rows_ref, msg_ref, n):
    count, levels = rows_ref.shape
    band_row = meta_ref[0:1, :]
    eye = iota((count, count), 0) == iota((count, count), 1)
    column = lambda row: jnp.sum(jnp.where(eye, row, 0.0), axis=1, keepdims=True)
    band_col, cell_col, top_col = (column(meta_ref[i : i + 1, :]) for i in range(3))
    same = band_row == band_col
    below = iota((count, count), 1) < iota((count, count), 0)
    above = iota((count, count), 1) > iota((count, count), 0)
    rank_col = jnp.sum(jnp.where(same & below, 1.0, 0.0), axis=1, keepdims=True)
    rank_row = jnp.sum(jnp.where(same & above, 1.0, 0.0), axis=0, keepdims=True)
    quad_col, quad_row = jnp.floor(rank_col * 0.125), jnp.floor(rank_row * 0.125)
    place_col, place_row = rank_col - 8.0 * quad_col, rank_row - 8.0 * quad_row
    slot = iota((n * 8, count), 0).astype(F32)
    lane = iota((count, 128), 1)
    wide = jnp.concatenate([rows_ref[...]] * QUADS, axis=1)
    keep = ((lane // levels).astype(F32) == quad_col) & ((lane % levels).astype(F32) < top_col)
    values = jnp.dot(
        jnp.where(band_row * 8.0 + place_row == slot, 1.0, 0.0),
        jnp.where(keep, wide, 0.0),
        precision=HIGHEST,
        preferred_element_type=F32,
    )
    mine = lax.rem(me * 8, 128)
    cells = jnp.dot(
        jnp.where(band_row * 8.0 + quad_row == slot, 1.0, 0.0),
        jnp.where((lane - mine).astype(F32) == place_col, cell_col, 0.0),
        precision=HIGHEST,
        preferred_element_type=F32,
    )
    msg_ref[:, 0:8, :] = values.reshape(n, 8, 128)
    msg_ref[:, 8:16, :] = cells.reshape(n, 8, 128)


def body(
    n, mems, owners, part_rows,
    meta_ref, rows_ref, perturb_ref, control_ref,
    out_ref,
    msg_ref, obs_ref, rhs_ref, cells_ref, inno_ref, v_ref, got_ref, m_ref, back_ref, g_hi, g_lo,
    obs_send, obs_recv, mem_send, mem_recv, v_send, v_recv, m_send, m_recv,
):
    me, mem = lax.axis_index("lat"), lax.axis_index("mem")
    lon, columns = out_ref.shape[1:]
    levels = rows_ref.shape[1]
    chunk = PARTS * part_rows

    barrier = pltpu.get_barrier_semaphore()

    def greet(k, carry):
        pl.semaphore_signal(barrier, inc=1, device_id={"lat": lax.rem(me + k, n)})
        return carry

    lax.fori_loop(1, n, greet, 0)
    for k in range(1, mems):
        pl.semaphore_signal(barrier, inc=1, device_id={"mem": lax.rem(mem + k, mems)})
    make_messages(me, meta_ref, rows_ref, msg_ref, n)
    pl.semaphore_wait(barrier, n - 1 + mems - 1)

    def obs_copy(k):
        there = lax.rem(me + k, n)
        return pltpu.make_async_remote_copy(
            src_ref=msg_ref.at[there], dst_ref=obs_ref.at[mem, me],
            send_sem=obs_send.at[k], recv_sem=obs_recv, device_id={"lat": there},
        )

    def start_obs(k, carry):
        obs_copy(k).start()
        return carry

    lax.fori_loop(1, n, start_obs, 0)
    obs_ref[mem, me] = msg_ref[me]
    local = obs_ref.at[mem, pl.ds(0, n - 1)]
    pltpu.make_async_copy(local, local, obs_recv).wait()

    def mem_copy(k):
        return pltpu.make_async_remote_copy(
            src_ref=obs_ref.at[mem], dst_ref=obs_ref.at[mem],
            send_sem=mem_send.at[k], recv_sem=mem_recv.at[k],
            device_id={"mem": lax.rem(mem + k, mems)},
        )

    for k in range(1, mems):
        mem_copy(k).start()
    for k in range(1, mems):
        mem_copy(k).wait()

    groups = n // 16
    group_slots = 128 * QUADS
    depth = mems * groups

    def stage(i, carry):
        m, t = i // groups, lax.rem(i, groups)
        source = pl.ds(t * 16, 16)
        rows = obs_ref[m, source, 0:8, :].reshape(128, 128)
        cells_ref[i] = jnp.sum(obs_ref[m, source, 8:16, :], axis=0)
        for q in range(QUADS):
            tiled = jnp.concatenate([rows[:, q * levels : (q + 1) * levels]] * QUADS, axis=1)
            high, low = split(tiled)
            rhs_ref[i, q * 128 : (q + 1) * 128, 0:128] = high
            rhs_ref[i, q * 128 : (q + 1) * 128, 128:256] = low
        return carry

    lax.fori_loop(0, depth, stage, 0)

    a, b = iota((columns, columns), 0), iota((columns, columns), 1)
    gap = (a % levels - b % levels).astype(F32)
    vert = jnp.where(a // levels == b // levels, jnp.exp(-0.5 * gap * gap), 0.0)
    vert_hi, vert_lo = split(vert)
    vert_both = jnp.concatenate([vert_hi, vert_hi], axis=0)

    block_rows = lon // BLOCKS
    block_owners = owners // BLOCKS

    def v_copy(dest, p):
        return pltpu.make_async_remote_copy(
            src_ref=v_ref.at[dest * PARTS + p], dst_ref=got_ref.at[p, me],
            send_sem=v_send.at[p, dest], recv_sem=v_recv.at[p], device_id={"lat": dest},
        )

    def send_block(block, p):
        def one(k, carry):
            dest = block * block_owners + lax.rem(me + k, block_owners)

            @pl.when(dest != me)
            def _():
                v_copy(dest, p).start()

            return carry

        lax.fori_loop(0, block_owners, one, 0)

    first = (me * BLOCKS) // n
    for step in range(BLOCKS):
        block = lax.rem(first + step, BLOCKS)
        base = block * block_rows
        position = (iota((block_rows, 128), 0) + base).astype(F32)

        def deposit(i):
            cells = cells_ref[i]
            hot = jnp.concatenate(
                [
                    jnp.where(position == cells[q : q + 1, :], 1.0, 0.0).astype(BF16)
                    for q in range(QUADS)
                ],
                axis=1,
            )
            return dot(hot, rhs_ref[i])

        inno_ref[...] = deposit(0)

        def more(i, carry):
            inno_ref[...] += deposit(i)
            return carry

        lax.fori_loop(1, depth, more, 0)
        innovation = inno_ref[:, 0:128] + inno_ref[:, 128:256]
        field = perturb_ref[0, pl.ds(pl.multiple_of(base, 16), block_rows), :].astype(F32)
        high, low = split(field * innovation)
        vertical = dot(jnp.concatenate([high, low], axis=1), vert_both) + dot(high, vert_lo)
        v_ref[pl.ds(block * (block_rows // part_rows), block_rows // part_rows)] = (
            vertical.reshape(block_rows // part_rows, part_rows, columns)
        )
        send_block(block, 0)
    for p in range(1, PARTS):
        for step in range(BLOCKS):
            send_block(lax.rem(first + step, BLOCKS), p)

    @pl.when(me < owners)
    def _():
        for p in range(PARTS):
            got_ref[p, me] = v_ref[me * PARTS + p]

    half = owners * part_rows
    spread = max(lon // 60, 4) / jnp.cos(
        1.2 * (jnp.full((1, half), me, jnp.int32).astype(F32) + 0.5) / n
    )
    scale = 1.0 / spread
    tile = 48

    def zonal_kernel(i, carry):
        start = pl.multiple_of(i * tile, tile)
        row = iota((tile, half), 0) + start
        for p in range(PARTS):
            k = iota((1, half), 1)
            col = (k // part_rows) * chunk + p * part_rows + k % part_rows
            distance = jnp.abs(row - col).astype(F32)
            distance = jnp.minimum(distance, lon - distance)
            ratio = distance * scale
            high, low = split(jnp.exp(-0.5 * (ratio * ratio)))
            g_hi[p, pl.ds(start, tile), :] = high
            g_lo[p, pl.ds(start, tile), :] = low
        return carry

    lax.fori_loop(0, lon // tile, zonal_kernel, 0)

    weights = [float(np.exp(np.float32(-0.5) * np.float32(d / 8.0) ** 2)) for d in range(n)]

    def m_copy(k, p):
        dest = lax.rem(me + k, n)
        return pltpu.make_async_remote_copy(
            src_ref=m_ref.at[p, dest], dst_ref=back_ref.at[p, me],
            send_sem=m_send.at[p, k], recv_sem=m_recv.at[p], device_id={"lat": dest},
        )

    @pl.when(me < owners)
    def _():
        for p in range(PARTS):
            arrived = got_ref.at[p, pl.ds(0, n - 1)]
            pltpu.make_async_copy(arrived, arrived, v_recv.at[p]).wait()

            def smooth(i, carry):
                rows = pl.ds(pl.multiple_of(i * 8, 8), 8)
                fields = [got_ref[p, r, rows, :] for r in range(n)]
                for r in range(n):
                    terms = [weights[abs(r - s)] * fields[s] for s in range(n)]
                    while len(terms) > 1:
                        terms = [terms[j] + terms[j + 1] for j in range(0, len(terms), 2)]
                    m_ref[p, r, rows, :] = terms[0]
                return carry

            lax.fori_loop(0, part_rows // 8, smooth, 0)

            def start_m(k, carry):
                m_copy(k, p).start()
                return carry

            lax.fori_loop(1, n, start_m, 0)
            back_ref[p, me] = m_ref[p, me]

    out_ref[0] = control_ref[0].astype(F32)
    for p in range(PARTS):
        for own, total in ((True, owners - 1), (False, owners)):

            @pl.when((me < owners) == own)
            def _():
                arrived = back_ref.at[p, pl.ds(0, total)]
                pltpu.make_async_copy(arrived, arrived, m_recv.at[p]).wait()

        high, low = split(back_ref[p].reshape(half, columns))
        both = jnp.concatenate([high, low], axis=1)
        for step in range(BLOCKS):
            rows = pl.ds(step * block_rows, block_rows)
            wide = dot(g_hi[p, rows, :], both)
            narrow = dot(g_lo[p, rows, :], high)
            out_ref[0, rows, :] += wide[:, 0:128] + (wide[:, 128:256] + narrow)

    def end_obs(k, carry):
        obs_copy(k).wait_send()
        return carry

    lax.fori_loop(1, n, end_obs, 0)
    for p in range(PARTS):

        def end_v(dest, carry):
            @pl.when(dest != me)
            def _():
                v_copy(dest, p).wait_send()

            return carry

        lax.fori_loop(0, owners, end_v, 0)

    @pl.when(me < owners)
    def _():
        for p in range(PARTS):

            def end_m(k, carry):
                m_copy(k, p).wait_send()
                return carry

            lax.fori_loop(1, n, end_m, 0)


def local(n, mems, obs_rows, obs_band, obs_cell, obs_top, perturb, control):
    _, lon, columns = perturb.shape
    count, levels = obs_rows.shape
    chunk = -(-lon // (n * 8 * PARTS)) * 8 * PARTS
    owners, part_rows = lon // chunk, chunk // PARTS
    assert owners * chunk == lon and owners % BLOCKS == 0 and owners <= n
    half = owners * part_rows
    depth = mems * n // 16
    meta = jnp.stack([obs_band.reshape(count), obs_cell, obs_top]).astype(F32)
    dma = pltpu.SemaphoreType.DMA
    return pl.pallas_call(
        functools.partial(body, n, mems, owners, part_rows),
        out_shape=jax.ShapeDtypeStruct((1, lon, columns), F32),
        in_specs=[pl.BlockSpec(memory_space=pltpu.VMEM)] * 4,
        out_specs=pl.BlockSpec(memory_space=pltpu.VMEM),
        scratch_shapes=[
            pltpu.VMEM((n, 16, 128), F32),
            pltpu.VMEM((mems, n, 16, 128), F32),
            pltpu.VMEM((depth, 128 * QUADS, 256), BF16),
            pltpu.VMEM((depth, 8, 128), F32),
            pltpu.VMEM((lon // BLOCKS, 256), F32),
            pltpu.VMEM((owners * PARTS, part_rows, columns), F32),
            pltpu.VMEM((PARTS, n, part_rows, columns), F32),
            pltpu.VMEM((PARTS, n, part_rows, columns), F32),
            pltpu.VMEM((PARTS, owners, part_rows, columns), F32),
            pltpu.VMEM((PARTS, lon, half), BF16),
            pltpu.VMEM((PARTS, lon, half), BF16),
            dma((n,)), dma(()), dma((mems,)), dma((mems,)),
            dma((PARTS, n)), dma((PARTS,)), dma((PARTS, n)), dma((PARTS,)),
        ],
        compiler_params=pltpu.CompilerParams(
            collective_id=0, has_side_effects=True, vmem_limit_bytes=56 * 1024 * 1024
        ),
    )(meta, obs_rows, perturb, control)


def solution(mesh):
    return jax.shard_map(
        functools.partial(local, mesh.shape["lat"], mesh.shape["mem"]),
        mesh=mesh,
        in_specs=(
            P(("lat", "mem"), None),
            P(("lat", "mem"), None),
            P(("lat", "mem")),
            P(("lat", "mem")),
            P("lat", None, "mem"),
            P("lat", None, "mem"),
        ),
        out_specs=P("lat", None, "mem"),
        check_vma=False,
    )
```

```python
import functools
import math

import jax
import jax.numpy as jnp
import numpy as np
from jax import lax
from jax.experimental import pallas as pl
from jax.experimental.pallas import tpu as pltpu
from jax.sharding import PartitionSpec as P

CAP = 32
PARTS = 3
BLOCKS = 3
QUADS = 4
F32 = jnp.float32
BF16 = jnp.bfloat16


def iota(shape, axis):
    return lax.broadcasted_iota(jnp.int32, shape, axis)


def split(value):
    high = value.astype(BF16)
    return high, (value - high.astype(F32)).astype(BF16)


def dot(left, right):
    return jnp.dot(left, right, preferred_element_type=F32)


def dot_nt(left, right):
    return lax.dot_general(left, right, (((1,), (1,)), ((), ())), preferred_element_type=F32)


def make_messages(me, rows_ref, band_ref, cell_ref, top_ref, msg_ref, n):
    levels, count = rows_ref.shape
    band = band_ref[...]
    named = iota((n, count), 0) == band
    before = iota((count, count), 0) < iota((count, count), 1)
    earlier = dot(
        jnp.where(named, 1.0, 0.0).astype(BF16), jnp.where(before, 1.0, 0.0).astype(BF16)
    )
    rank = jnp.sum(jnp.where(named, earlier, 0.0), axis=0, keepdims=True).astype(jnp.int32)
    quad, place = rank // 8, rank % 8
    slot = iota((n * 8, count), 0)
    line = iota((128, count), 0)
    wide = jnp.concatenate([rows_ref[...]] * QUADS, axis=0)
    keep = (line // levels == quad) & (line % levels < top_ref[...])
    high, low = split(jnp.where(keep, wide, 0.0))
    values = dot_nt(
        jnp.where(band * 8 + place == slot, 1.0, 0.0).astype(BF16),
        jnp.concatenate([high, low], axis=0),
    )
    mine = lax.rem(me * 8, 128)
    high, low = split(jnp.where(line - mine == place, cell_ref[...].astype(F32), 0.0))
    cells = dot_nt(
        jnp.where(band * 8 + quad == slot, 1.0, 0.0).astype(BF16),
        jnp.concatenate([high, low], axis=0),
    )
    msg_ref[:, 0:8, :] = (values[:, 0:128] + values[:, 128:256]).reshape(n, 8, 128)
    msg_ref[:, 8:16, :] = (cells[:, 0:128] + cells[:, 128:256]).reshape(n, 8, 128)


def body(
    n, mems, owners, part_rows,
    rows_ref, band_ref, cell_ref, top_ref, perturb_ref,
    out_ref,
    msg_ref, obs_ref, rhs_ref, cells_ref, inno_ref, v_ref, got_ref, m_ref, back_ref, g_hi, g_lo,
    obs_send, obs_recv, mem_send, mem_recv, v_send, v_recv, m_send, m_recv,
):
    me, mem = lax.axis_index("lat"), lax.axis_index("mem")
    lon, columns = out_ref.shape[1:]
    levels = rows_ref.shape[0]
    chunk = PARTS * part_rows

    barrier = pltpu.get_barrier_semaphore()

    def greet(k, carry):
        pl.semaphore_signal(barrier, inc=1, device_id={"lat": lax.rem(me + k, n)})
        return carry

    lax.fori_loop(1, n, greet, 0)
    for k in range(1, mems):
        pl.semaphore_signal(barrier, inc=1, device_id={"mem": lax.rem(mem + k, mems)})
    make_messages(me, rows_ref, band_ref, cell_ref, top_ref, msg_ref, n)
    pl.semaphore_wait(barrier, n - 1 + mems - 1)

    def obs_copy(k):
        there = lax.rem(me + k, n)
        return pltpu.make_async_remote_copy(
            src_ref=msg_ref.at[there], dst_ref=obs_ref.at[mem, me],
            send_sem=obs_send.at[k], recv_sem=obs_recv, device_id={"lat": there},
        )

    def start_obs(k, carry):
        obs_copy(k).start()
        return carry

    lax.fori_loop(1, n, start_obs, 0)
    obs_ref[mem, me] = msg_ref[me]

    half = owners * part_rows
    tile = 48

    def zonal_kernel(p):
        spread = max(lon // 60, 4) / jnp.cos(
            1.2 * (jnp.full((1, half), me, jnp.int32).astype(F32) + 0.5) / n
        )
        scale = 1.0 / spread
        k = iota((1, half), 1)
        col = (k // part_rows) * chunk + p * part_rows + k % part_rows

        def rows_of(i, carry):
            start = pl.multiple_of(i * tile, tile)
            distance = jnp.abs(iota((tile, half), 0) + start - col).astype(F32)
            ratio = jnp.minimum(distance, lon - distance) * scale
            high, low = split(jnp.exp(-0.5 * (ratio * ratio)))
            g_hi[p, pl.ds(start, tile), :] = high
            g_lo[p, pl.ds(start, tile), :] = low
            return carry

        lax.fori_loop(0, lon // tile, rows_of, 0)

    zonal_kernel(0)
    a, b = iota((columns, columns), 0), iota((columns, columns), 1)
    gap = (a % levels - b % levels).astype(F32)
    vert = jnp.where(a // levels == b // levels, jnp.exp(-0.5 * gap * gap), 0.0)
    vert_hi, vert_lo = split(vert)
    vert_both = jnp.concatenate([vert_hi, vert_hi], axis=0)

    local = obs_ref.at[mem, pl.ds(0, n - 1)]
    pltpu.make_async_copy(local, local, obs_recv).wait()

    def mem_copy(k):
        return pltpu.make_async_remote_copy(
            src_ref=obs_ref.at[mem], dst_ref=obs_ref.at[mem],
            send_sem=mem_send.at[k], recv_sem=mem_recv.at[k],
            device_id={"mem": lax.rem(mem + k, mems)},
        )

    for k in range(1, mems):
        mem_copy(k).start()
    for k in range(1, mems):
        mem_copy(k).wait()

    groups = n // 16
    group_slots = 128 * QUADS
    depth = mems * groups

    def stage(i, carry):
        m, t = i // groups, lax.rem(i, groups)
        source = pl.ds(t * 16, 16)
        rows = obs_ref[m, source, 0:8, :].reshape(128, 128)
        cells_ref[i] = jnp.sum(obs_ref[m, source, 8:16, :], axis=0)
        for q in range(QUADS):
            tiled = jnp.concatenate([rows[:, q * levels : (q + 1) * levels]] * QUADS, axis=1)
            high, low = split(tiled)
            rhs_ref[i, q * 128 : (q + 1) * 128, 0:128] = high
            rhs_ref[i, q * 128 : (q + 1) * 128, 128:256] = low
        return carry

    lax.fori_loop(0, depth, stage, 0)

    block_rows = lon // BLOCKS
    block_owners = owners // BLOCKS

    def v_copy(dest, p):
        return pltpu.make_async_remote_copy(
            src_ref=v_ref.at[dest * PARTS + p], dst_ref=got_ref.at[p, me],
            send_sem=v_send.at[p, dest], recv_sem=v_recv.at[p], device_id={"lat": dest},
        )

    def send_block(block, p):
        def one(k, carry):
            dest = block * block_owners + lax.rem(me + k, block_owners)

            @pl.when(dest != me)
            def _():
                v_copy(dest, p).start()

            return carry

        lax.fori_loop(0, block_owners, one, 0)

    mid = n // 2
    lower = me < mid

    def order(k):
        low_half = lower == (k >= mid)
        return jnp.where(low_half, 0, mid) + lax.rem(me + k, mid)

    for step in range(BLOCKS):
        block = jnp.where(lower, BLOCKS - 1 - step, step)
        base = block * block_rows
        position = (iota((block_rows, 128), 0) + base).astype(F32)

        def deposit(i):
            cells = cells_ref[i]
            hot = jnp.concatenate(
                [
                    jnp.where(position == cells[q : q + 1, :], 1.0, 0.0).astype(BF16)
                    for q in range(QUADS)
                ],
                axis=1,
            )
            return dot(hot, rhs_ref[i])

        inno_ref[...] = deposit(0)

        def more(i, carry):
            inno_ref[...] += deposit(i)
            return carry

        lax.fori_loop(1, depth, more, 0)
        innovation = inno_ref[:, 0:128] + inno_ref[:, 128:256]
        field = perturb_ref[0, pl.ds(pl.multiple_of(base, 16), block_rows), :].astype(F32)
        high, low = split(field * innovation)
        vertical = dot(jnp.concatenate([high, low], axis=1), vert_both) + dot(high, vert_lo)
        v_ref[pl.ds(block * (block_rows // part_rows), block_rows // part_rows)] = (
            vertical.reshape(block_rows // part_rows, part_rows, columns)
        )
        send_block(block, 0)
    for p in range(1, PARTS):


        def send_part(k, carry):
            dest = order(k)

            @pl.when((dest != me) & (dest < owners))
            def _():
                v_copy(dest, p).start()

            return carry

        lax.fori_loop(0, n, send_part, 0)

    @pl.when(me < owners)
    def _():
        for p in range(PARTS):
            got_ref[p, me] = v_ref[me * PARTS + p]

    for p in range(1, PARTS):
        zonal_kernel(p)

    weights = [float(np.exp(np.float32(-0.5) * np.float32(d / 8.0) ** 2)) for d in range(n)]

    def m_copy(k, p):
        dest = order(k)
        return pltpu.make_async_remote_copy(
            src_ref=m_ref.at[p, dest], dst_ref=back_ref.at[p, me],
            send_sem=m_send.at[p, k], recv_sem=m_recv.at[p], device_id={"lat": dest},
        )

    @pl.when(me < owners)
    def _():
        for p in range(PARTS):
            arrived = got_ref.at[p, pl.ds(0, n - 1)]
            pltpu.make_async_copy(arrived, arrived, v_recv.at[p]).wait()

            def smooth(i, carry):
                rows = pl.ds(pl.multiple_of(i * 8, 8), 8)
                fields = [got_ref[p, r, rows, :] for r in range(n)]
                for r in range(n):
                    terms = [weights[abs(r - s)] * fields[s] for s in range(n)]
                    while len(terms) > 1:
                        terms = [terms[j] + terms[j + 1] for j in range(0, len(terms), 2)]
                    m_ref[p, r, rows, :] = terms[0]
                return carry

            lax.fori_loop(0, part_rows // 8, smooth, 0)

            def start_m(k, carry):
                m_copy(k, p).start()
                return carry

            lax.fori_loop(0, mid, start_m, 0)
            lax.fori_loop(mid + 1, n, start_m, 0)
            back_ref[p, me] = m_ref[p, me]

    for p in range(PARTS):
        for own, total in ((True, owners - 1), (False, owners)):

            @pl.when((me < owners) == own)
            def _():
                arrived = back_ref.at[p, pl.ds(0, total)]
                pltpu.make_async_copy(arrived, arrived, m_recv.at[p]).wait()

        high, low = split(back_ref[p].reshape(half, columns))
        both = jnp.concatenate([high, low], axis=1)
        for step in range(BLOCKS):
            rows = pl.ds(step * block_rows, block_rows)
            wide = dot(g_hi[p, rows, :], both)
            narrow = dot(g_lo[p, rows, :], high)
            total = wide[:, 0:128] + (wide[:, 128:256] + narrow)
            out_ref[0, rows, :] = total if p == 0 else out_ref[0, rows, :] + total

    def end_obs(k, carry):
        obs_copy(k).wait_send()
        return carry

    lax.fori_loop(1, n, end_obs, 0)
    for p in range(PARTS):

        def end_v(dest, carry):
            @pl.when(dest != me)
            def _():
                v_copy(dest, p).wait_send()

            return carry

        lax.fori_loop(0, owners, end_v, 0)

    @pl.when(me < owners)
    def _():
        for p in range(PARTS):

            def end_m(k, carry):
                m_copy(k, p).wait_send()
                return carry

            lax.fori_loop(0, mid, end_m, 0)
            lax.fori_loop(mid + 1, n, end_m, 0)


def local(n, mems, obs_rows, obs_band, obs_cell, obs_top, perturb, control):
    _, lon, columns = perturb.shape
    count, levels = obs_rows.shape
    chunk = -(-lon // (n * 8 * PARTS)) * 8 * PARTS
    owners, part_rows = lon // chunk, chunk // PARTS
    assert owners * chunk == lon and owners % BLOCKS == 0 and owners <= n
    half = owners * part_rows
    depth = mems * n // 16
    dma = pltpu.SemaphoreType.DMA
    zonal = pl.pallas_call(
        functools.partial(body, n, mems, owners, part_rows),
        out_shape=jax.ShapeDtypeStruct((1, lon, columns), F32),
        in_specs=[pl.BlockSpec(memory_space=pltpu.VMEM)] * 5,
        out_specs=pl.BlockSpec(memory_space=pltpu.VMEM),
        scratch_shapes=[
            pltpu.VMEM((n, 16, 128), F32),
            pltpu.VMEM((mems, n, 16, 128), F32),
            pltpu.VMEM((depth, 128 * QUADS, 256), BF16),
            pltpu.VMEM((depth, 8, 128), F32),
            pltpu.VMEM((lon // BLOCKS, 256), F32),
            pltpu.VMEM((owners * PARTS, part_rows, columns), F32),
            pltpu.VMEM((PARTS, n, part_rows, columns), F32),
            pltpu.VMEM((PARTS, n, part_rows, columns), F32),
            pltpu.VMEM((PARTS, owners, part_rows, columns), F32),
            pltpu.VMEM((PARTS, lon, half), BF16),
            pltpu.VMEM((PARTS, lon, half), BF16),
            dma((n,)), dma(()), dma((mems,)), dma((mems,)),
            dma((PARTS, n)), dma((PARTS,)), dma((PARTS, n)), dma((PARTS,)),
        ],
        compiler_params=pltpu.CompilerParams(
            collective_id=0, has_side_effects=True, vmem_limit_bytes=30 * 1024 * 1024
        ),
    )(
        obs_rows.T, obs_band.reshape(1, count), obs_cell.reshape(1, count),
        obs_top.reshape(1, count), perturb,
    )
    return control.astype(F32) + zonal


def solution(mesh):
    return jax.shard_map(
        functools.partial(local, mesh.shape["lat"], mesh.shape["mem"]),
        mesh=mesh,
        in_specs=(
            P(("lat", "mem"), None),
            P(("lat", "mem"), None),
            P(("lat", "mem")),
            P(("lat", "mem")),
            P("lat", None, "mem"),
            P("lat", None, "mem"),
        ),
        out_specs=P("lat", None, "mem"),
        check_vma=False,
    )
```

```python
import functools
import math

import jax
import jax.numpy as jnp
import numpy as np
from jax import lax
from jax.experimental import pallas as pl
from jax.experimental.pallas import tpu as pltpu
from jax.sharding import PartitionSpec as P

CAP = 32
PARTS = 3
BLOCKS = 3
QUADS = 4
F32 = jnp.float32
BF16 = jnp.bfloat16


def iota(shape, axis):
    return lax.broadcasted_iota(jnp.int32, shape, axis)


def split(value):
    high = value.astype(BF16)
    return high, (value - high.astype(F32)).astype(BF16)


def dot(left, right):
    return jnp.dot(left, right, preferred_element_type=F32)


def dot_nt(left, right):
    return lax.dot_general(left, right, (((1,), (1,)), ((), ())), preferred_element_type=F32)


def make_messages(me, rows_ref, band_ref, cell_ref, top_ref, msg_ref, n):
    levels, count = rows_ref.shape
    band = band_ref[...]
    named = iota((n, count), 0) == band
    before = iota((count, count), 0) < iota((count, count), 1)
    earlier = dot(
        jnp.where(named, 1.0, 0.0).astype(BF16), jnp.where(before, 1.0, 0.0).astype(BF16)
    )
    rank = jnp.sum(jnp.where(named, earlier, 0.0), axis=0, keepdims=True).astype(jnp.int32)
    quad, place = rank // 8, rank % 8
    slot = iota((n * 8, count), 0)
    line = iota((128, count), 0)
    wide = jnp.concatenate([rows_ref[...]] * QUADS, axis=0)
    keep = (line // levels == quad) & (line % levels < top_ref[...])
    high, low = split(jnp.where(keep, wide, 0.0))
    values = dot_nt(
        jnp.where(band * 8 + place == slot, 1.0, 0.0).astype(BF16),
        jnp.concatenate([high, low], axis=0),
    )
    mine = lax.rem(me * 8, 128)
    high, low = split(jnp.where(line - mine == place, cell_ref[...].astype(F32), 0.0))
    cells = dot_nt(
        jnp.where(band * 8 + quad == slot, 1.0, 0.0).astype(BF16),
        jnp.concatenate([high, low], axis=0),
    )
    msg_ref[:, 0:8, :] = (values[:, 0:128] + values[:, 128:256]).reshape(n, 8, 128)
    msg_ref[:, 8:16, :] = (cells[:, 0:128] + cells[:, 128:256]).reshape(n, 8, 128)


def body(
    n, mems, owners, part_rows,
    rows_hbm, band_hbm, cell_hbm, top_hbm, perturb_hbm,
    out_ref,
    rows_ref, band_ref, cell_ref, top_ref, perturb_ref, in_sem,
    msg_ref, obs_ref, rhs_ref, cells_ref, inno_ref, v_ref, got_ref, m_ref, back_ref, g_hi, g_lo, both_ref,
    obs_send, obs_recv, mem_send, mem_recv, v_send, v_recv, m_send, m_recv,
):
    me, mem = lax.axis_index("lat"), lax.axis_index("mem")
    lon, columns = out_ref.shape[1:]
    levels = rows_ref.shape[0]
    chunk = PARTS * part_rows

    loads = [
        pltpu.make_async_copy(source, target, in_sem.at[i])
        for i, (source, target) in enumerate(
            (
                (rows_hbm, rows_ref), (band_hbm, band_ref), (cell_hbm, cell_ref),
                (top_hbm, top_ref), (perturb_hbm, perturb_ref),
            )
        )
    ]
    for load in loads:
        load.start()
    barrier = pltpu.get_barrier_semaphore()

    def greet(k, carry):
        pl.semaphore_signal(barrier, inc=1, device_id={"lat": lax.rem(me + k, n)})
        return carry

    lax.fori_loop(1, n, greet, 0)
    for k in range(1, mems):
        pl.semaphore_signal(barrier, inc=1, device_id={"mem": lax.rem(mem + k, mems)})
    for load in loads[:4]:
        load.wait()
    make_messages(me, rows_ref, band_ref, cell_ref, top_ref, msg_ref, n)
    pl.semaphore_wait(barrier, n - 1 + mems - 1)

    def obs_copy(k):
        there = lax.rem(me + k, n)
        return pltpu.make_async_remote_copy(
            src_ref=msg_ref.at[there], dst_ref=obs_ref.at[mem, me],
            send_sem=obs_send.at[k], recv_sem=obs_recv, device_id={"lat": there},
        )

    def start_obs(k, carry):
        obs_copy(k).start()
        return carry

    lax.fori_loop(1, n, start_obs, 0)
    obs_ref[mem, me] = msg_ref[me]

    half = owners * part_rows
    tile = 48

    def zonal_kernel(p):
        spread = max(lon // 60, 4) / jnp.cos(
            1.2 * (jnp.full((1, half), me, jnp.int32).astype(F32) + 0.5) / n
        )
        scale = 1.0 / spread
        k = iota((1, half), 1)
        col = (k // part_rows) * chunk + p * part_rows + k % part_rows

        def rows_of(i, carry):
            start = pl.multiple_of(i * tile, tile)
            distance = jnp.abs(iota((tile, half), 0) + start - col).astype(F32)
            ratio = jnp.minimum(distance, lon - distance) * scale
            high, low = split(jnp.exp(-0.5 * (ratio * ratio)))
            g_hi[p, pl.ds(start, tile), :] = high
            g_lo[p, pl.ds(start, tile), :] = low
            return carry

        lax.fori_loop(0, lon // BLOCKS // tile, rows_of, 0)

    zonal_kernel(0)
    a, b = iota((columns, columns), 0), iota((columns, columns), 1)
    gap = (a % levels - b % levels).astype(F32)
    vert = jnp.where(a // levels == b // levels, jnp.exp(-0.5 * gap * gap), 0.0)
    vert_hi, vert_lo = split(vert)
    vert_both = jnp.concatenate([vert_hi, vert_hi], axis=0)

    local = obs_ref.at[mem, pl.ds(0, n - 1)]
    pltpu.make_async_copy(local, local, obs_recv).wait()

    def mem_copy(k):
        return pltpu.make_async_remote_copy(
            src_ref=obs_ref.at[mem], dst_ref=obs_ref.at[mem],
            send_sem=mem_send.at[k], recv_sem=mem_recv.at[k],
            device_id={"mem": lax.rem(mem + k, mems)},
        )

    for k in range(1, mems):
        mem_copy(k).start()
    for k in range(1, mems):
        mem_copy(k).wait()

    groups = n // 16
    group_slots = 128 * QUADS
    depth = mems * groups

    def stage(i, carry):
        m, t = i // groups, lax.rem(i, groups)
        source = pl.ds(t * 16, 16)
        rows = obs_ref[m, source, 0:8, :].reshape(128, 128)
        cells_ref[i] = jnp.sum(obs_ref[m, source, 8:16, :], axis=0)
        for q in range(QUADS):
            tiled = jnp.concatenate([rows[:, q * levels : (q + 1) * levels]] * QUADS, axis=1)
            high, low = split(tiled)
            rhs_ref[i, q * 128 : (q + 1) * 128, 0:128] = high
            rhs_ref[i, q * 128 : (q + 1) * 128, 128:256] = low
        return carry

    lax.fori_loop(0, depth, stage, 0)

    block_rows = lon // BLOCKS
    block_owners = owners // BLOCKS

    def v_copy(dest, p):
        return pltpu.make_async_remote_copy(
            src_ref=v_ref.at[dest * PARTS + p], dst_ref=got_ref.at[p, me],
            send_sem=v_send.at[p, dest], recv_sem=v_recv.at[p], device_id={"lat": dest},
        )

    def send_block(block, p):
        def one(k, carry):
            dest = block * block_owners + lax.rem(me + k, block_owners)

            @pl.when(dest != me)
            def _():
                v_copy(dest, p).start()

            return carry

        lax.fori_loop(0, block_owners, one, 0)

    mid = n // 2
    lower = me < mid

    def order(k):
        low_half = lower == (k >= mid)
        return jnp.where(low_half, 0, mid) + lax.rem(me + k, mid)

    loads[4].wait()
    for step in range(BLOCKS):
        block = jnp.where(lower, BLOCKS - 1 - step, step)
        base = block * block_rows
        position = (iota((block_rows, 128), 0) + base).astype(F32)

        def deposit(i):
            cells = cells_ref[i]
            hot = jnp.concatenate(
                [
                    jnp.where(position == cells[q : q + 1, :], 1.0, 0.0).astype(BF16)
                    for q in range(QUADS)
                ],
                axis=1,
            )
            return dot(hot, rhs_ref[i])

        inno_ref[...] = deposit(0)

        def more(i, carry):
            inno_ref[...] += deposit(i)
            return carry

        lax.fori_loop(1, depth, more, 0)
        innovation = inno_ref[:, 0:128] + inno_ref[:, 128:256]
        field = perturb_ref[0, pl.ds(pl.multiple_of(base, 16), block_rows), :].astype(F32)
        high, low = split(field * innovation)
        vertical = dot(jnp.concatenate([high, low], axis=1), vert_both) + dot(high, vert_lo)
        v_ref[pl.ds(block * (block_rows // part_rows), block_rows // part_rows)] = (
            vertical.reshape(block_rows // part_rows, part_rows, columns)
        )
        send_block(block, 0)
    for p in range(1, PARTS):


        def send_part(k, carry):
            dest = order(k)

            @pl.when((dest != me) & (dest < owners))
            def _():
                v_copy(dest, p).start()

            return carry

        lax.fori_loop(0, n, send_part, 0)

    @pl.when(me < owners)
    def _():
        for p in range(PARTS):
            got_ref[p, me] = v_ref[me * PARTS + p]

    for p in range(1, PARTS):
        zonal_kernel(p)

    weights = [float(np.exp(np.float32(-0.5) * np.float32(d / 8.0) ** 2)) for d in range(n)]

    def m_copy(k, p):
        dest = order(k)
        return pltpu.make_async_remote_copy(
            src_ref=m_ref.at[p, dest], dst_ref=back_ref.at[p, me],
            send_sem=m_send.at[p, k], recv_sem=m_recv.at[p], device_id={"lat": dest},
        )

    @pl.when(me < owners)
    def _():
        for p in range(PARTS):
            arrived = got_ref.at[p, pl.ds(0, n - 1)]
            pltpu.make_async_copy(arrived, arrived, v_recv.at[p]).wait()

            def smooth(i, carry):
                rows = pl.ds(pl.multiple_of(i * 8, 8), 8)
                fields = [got_ref[p, r, rows, :] for r in range(n)]
                for r in range(n):
                    terms = [weights[abs(r - s)] * fields[s] for s in range(n)]
                    while len(terms) > 1:
                        terms = [terms[j] + terms[j + 1] for j in range(0, len(terms), 2)]
                    m_ref[p, r, rows, :] = terms[0]
                return carry

            lax.fori_loop(0, part_rows // 8, smooth, 0)

            def start_m(k, carry):
                m_copy(k, p).start()
                return carry

            lax.fori_loop(0, mid, start_m, 0)
            lax.fori_loop(mid + 1, n, start_m, 0)
            back_ref[p, me] = m_ref[p, me]

    for p in range(PARTS):
        for own, total in ((True, owners - 1), (False, owners)):

            @pl.when((me < owners) == own)
            def _():
                arrived = back_ref.at[p, pl.ds(0, total)]
                pltpu.make_async_copy(arrived, arrived, m_recv.at[p]).wait()

        both = jnp.concatenate(split(back_ref[p].reshape(half, columns)), axis=1)
        both_ref[p, 0:half, :] = both
        both_ref[p, half : 2 * half, :] = both
        for step in range(BLOCKS):
            rows = pl.ds(step * block_rows, block_rows)
            turn = pl.ds(step * (half // BLOCKS), half)
            wide = dot(g_hi[p], both_ref[p, turn, :])
            narrow = dot(g_lo[p], both_ref[p, turn, 0:128])
            total = wide[:, 0:128] + (wide[:, 128:256] + narrow)
            out_ref[0, rows, :] = total if p == 0 else out_ref[0, rows, :] + total

    def end_obs(k, carry):
        obs_copy(k).wait_send()
        return carry

    lax.fori_loop(1, n, end_obs, 0)
    for p in range(PARTS):

        def end_v(dest, carry):
            @pl.when(dest != me)
            def _():
                v_copy(dest, p).wait_send()

            return carry

        lax.fori_loop(0, owners, end_v, 0)

    @pl.when(me < owners)
    def _():
        for p in range(PARTS):

            def end_m(k, carry):
                m_copy(k, p).wait_send()
                return carry

            lax.fori_loop(0, mid, end_m, 0)
            lax.fori_loop(mid + 1, n, end_m, 0)


def local(n, mems, obs_rows, obs_band, obs_cell, obs_top, perturb, control):
    _, lon, columns = perturb.shape
    count, levels = obs_rows.shape
    chunk = -(-lon // (n * 8 * PARTS)) * 8 * PARTS
    owners, part_rows = lon // chunk, chunk // PARTS
    assert owners * chunk == lon and owners % BLOCKS == 0 and owners <= n
    half = owners * part_rows
    depth = mems * n // 16
    dma = pltpu.SemaphoreType.DMA
    zonal = pl.pallas_call(
        functools.partial(body, n, mems, owners, part_rows),
        out_shape=jax.ShapeDtypeStruct((1, lon, columns), F32),
        in_specs=[pl.BlockSpec(memory_space=pltpu.HBM)] * 5,
        out_specs=pl.BlockSpec(memory_space=pltpu.VMEM),
        scratch_shapes=[
            pltpu.VMEM((levels, count), F32),
            pltpu.VMEM((1, count), jnp.int32),
            pltpu.VMEM((1, count), jnp.int32),
            pltpu.VMEM((1, count), jnp.int32),
            pltpu.VMEM((1, lon, columns), BF16),
            pltpu.SemaphoreType.DMA((5,)),
            pltpu.VMEM((n, 16, 128), F32),
            pltpu.VMEM((mems, n, 16, 128), F32),
            pltpu.VMEM((depth, 128 * QUADS, 256), BF16),
            pltpu.VMEM((depth, 8, 128), F32),
            pltpu.VMEM((lon // BLOCKS, 256), F32),
            pltpu.VMEM((owners * PARTS, part_rows, columns), F32),
            pltpu.VMEM((PARTS, n, part_rows, columns), F32),
            pltpu.VMEM((PARTS, n, part_rows, columns), F32),
            pltpu.VMEM((PARTS, owners, part_rows, columns), F32),
            pltpu.VMEM((PARTS, lon // BLOCKS, half), BF16),
            pltpu.VMEM((PARTS, lon // BLOCKS, half), BF16),
            pltpu.VMEM((PARTS, 2 * half, 256), BF16),
            dma((n,)), dma(()), dma((mems,)), dma((mems,)),
            dma((PARTS, n)), dma((PARTS,)), dma((PARTS, n)), dma((PARTS,)),
        ],
        compiler_params=pltpu.CompilerParams(
            collective_id=0, has_side_effects=True, vmem_limit_bytes=56 * 1024 * 1024
        ),
    )(
        obs_rows.T, obs_band.reshape(1, count), obs_cell.reshape(1, count),
        obs_top.reshape(1, count), perturb,
    )
    return control.astype(F32) + zonal


def solution(mesh):
    return jax.shard_map(
        functools.partial(local, mesh.shape["lat"], mesh.shape["mem"]),
        mesh=mesh,
        in_specs=(
            P(("lat", "mem"), None),
            P(("lat", "mem"), None),
            P(("lat", "mem")),
            P(("lat", "mem")),
            P("lat", None, "mem"),
            P("lat", None, "mem"),
        ),
        out_specs=P("lat", None, "mem"),
        check_vma=False,
    )
```

```python
import functools
import math

import jax
import jax.numpy as jnp
import numpy as np
from jax import lax
from jax.experimental import pallas as pl
from jax.experimental.pallas import tpu as pltpu
from jax.sharding import PartitionSpec as P

CAP = 32
PARTS = 6
BLOCKS = 3
QUADS = 4
F32 = jnp.float32
BF16 = jnp.bfloat16


def iota(shape, axis):
    return lax.broadcasted_iota(jnp.int32, shape, axis)


def split(value):
    high = value.astype(BF16)
    return high, (value - high.astype(F32)).astype(BF16)


def dot(left, right):
    return jnp.dot(left, right, preferred_element_type=F32)


def dot_nt(left, right):
    return lax.dot_general(left, right, (((1,), (1,)), ((), ())), preferred_element_type=F32)


def make_messages(me, rows_ref, band_ref, cell_ref, top_ref, msg_ref, n):
    levels, count = rows_ref.shape
    band = band_ref[...]
    named = iota((n, count), 0) == band
    before = iota((count, count), 0) < iota((count, count), 1)
    earlier = dot(
        jnp.where(named, 1.0, 0.0).astype(BF16), jnp.where(before, 1.0, 0.0).astype(BF16)
    )
    rank = jnp.sum(jnp.where(named, earlier, 0.0), axis=0, keepdims=True).astype(jnp.int32)
    quad, place = rank // 8, rank % 8
    slot = iota((n * 8, count), 0)
    line = iota((128, count), 0)
    wide = jnp.concatenate([rows_ref[...]] * QUADS, axis=0)
    keep = (line // levels == quad) & (line % levels < top_ref[...])
    high, low = split(jnp.where(keep, wide, 0.0))
    values = dot_nt(
        jnp.where(band * 8 + place == slot, 1.0, 0.0).astype(BF16),
        jnp.concatenate([high, low], axis=0),
    )
    mine = lax.rem(me * 8, 128)
    high, low = split(jnp.where(line - mine == place, cell_ref[...].astype(F32), 0.0))
    cells = dot_nt(
        jnp.where(band * 8 + quad == slot, 1.0, 0.0).astype(BF16),
        jnp.concatenate([high, low], axis=0),
    )
    msg_ref[:, 0:8, :] = (values[:, 0:128] + values[:, 128:256]).reshape(n, 8, 128)
    msg_ref[:, 8:16, :] = (cells[:, 0:128] + cells[:, 128:256]).reshape(n, 8, 128)


def body(
    n, mems, owners, part_rows,
    rows_hbm, band_hbm, cell_hbm, top_hbm, perturb_hbm,
    out_ref,
    rows_ref, band_ref, cell_ref, top_ref, perturb_ref, in_sem,
    msg_ref, obs_ref, rhs_ref, cells_ref, inno_ref, v_ref, got_ref, m_ref, back_ref, g_hi, g_lo, both_ref, sum_ref, out_sem,
    obs_send, obs_recv, mem_send, mem_recv, v_send, v_recv, m_send, m_recv,
):
    me, mem = lax.axis_index("lat"), lax.axis_index("mem")
    lon, columns = out_ref.shape[1:]
    levels = rows_ref.shape[0]
    chunk = PARTS * part_rows

    loads = [
        pltpu.make_async_copy(source, target, in_sem.at[i])
        for i, (source, target) in enumerate(
            (
                (rows_hbm, rows_ref), (band_hbm, band_ref), (cell_hbm, cell_ref),
                (top_hbm, top_ref), (perturb_hbm, perturb_ref),
            )
        )
    ]
    for load in loads:
        load.start()
    barrier = pltpu.get_barrier_semaphore()

    def greet(k, carry):
        pl.semaphore_signal(barrier, inc=1, device_id={"lat": lax.rem(me + k, n)})
        return carry

    lax.fori_loop(1, n, greet, 0)
    for k in range(1, mems):
        pl.semaphore_signal(barrier, inc=1, device_id={"mem": lax.rem(mem + k, mems)})
    for load in loads[:4]:
        load.wait()
    make_messages(me, rows_ref, band_ref, cell_ref, top_ref, msg_ref, n)
    pl.semaphore_wait(barrier, n - 1 + mems - 1)

    def obs_copy(k):
        there = lax.rem(me + k, n)
        return pltpu.make_async_remote_copy(
            src_ref=msg_ref.at[there], dst_ref=obs_ref.at[mem, me],
            send_sem=obs_send.at[k], recv_sem=obs_recv, device_id={"lat": there},
        )

    def start_obs(k, carry):
        obs_copy(k).start()
        return carry

    lax.fori_loop(1, n, start_obs, 0)
    obs_ref[mem, me] = msg_ref[me]

    half = owners * part_rows
    tile = 48

    def zonal_kernel(p):
        spread = max(lon // 60, 4) / jnp.cos(
            1.2 * (jnp.full((1, half), me, jnp.int32).astype(F32) + 0.5) / n
        )
        scale = 1.0 / spread
        k = iota((1, half), 1)
        col = (k // part_rows) * chunk + p * part_rows + k % part_rows

        def rows_of(i, carry):
            start = pl.multiple_of(i * tile, tile)
            distance = jnp.abs(iota((tile, half), 0) + start - col).astype(F32)
            ratio = jnp.minimum(distance, lon - distance) * scale
            high, low = split(jnp.exp(-0.5 * (ratio * ratio)))
            g_hi[p, pl.ds(start, tile), :] = high
            g_lo[p, pl.ds(start, tile), :] = low
            return carry

        lax.fori_loop(0, lon // BLOCKS // tile, rows_of, 0)

    zonal_kernel(0)
    a, b = iota((columns, columns), 0), iota((columns, columns), 1)
    gap = (a % levels - b % levels).astype(F32)
    vert = jnp.where(a // levels == b // levels, jnp.exp(-0.5 * gap * gap), 0.0)
    vert_hi, vert_lo = split(vert)
    vert_both = jnp.concatenate([vert_hi, vert_hi], axis=0)

    local = obs_ref.at[mem, pl.ds(0, n - 1)]
    pltpu.make_async_copy(local, local, obs_recv).wait()

    def mem_copy(k):
        return pltpu.make_async_remote_copy(
            src_ref=obs_ref.at[mem], dst_ref=obs_ref.at[mem],
            send_sem=mem_send.at[k], recv_sem=mem_recv.at[k],
            device_id={"mem": lax.rem(mem + k, mems)},
        )

    for k in range(1, mems):
        mem_copy(k).start()
    for k in range(1, mems):
        mem_copy(k).wait()

    groups = n // 16
    group_slots = 128 * QUADS
    depth = mems * groups

    def stage(i, carry):
        m, t = i // groups, lax.rem(i, groups)
        source = pl.ds(t * 16, 16)
        rows = obs_ref[m, source, 0:8, :].reshape(128, 128)
        cells_ref[i] = jnp.sum(obs_ref[m, source, 8:16, :], axis=0)
        for q in range(QUADS):
            tiled = jnp.concatenate([rows[:, q * levels : (q + 1) * levels]] * QUADS, axis=1)
            high, low = split(tiled)
            rhs_ref[i, q * 128 : (q + 1) * 128, 0:128] = high
            rhs_ref[i, q * 128 : (q + 1) * 128, 128:256] = low
        return carry

    lax.fori_loop(0, depth, stage, 0)

    block_rows = lon // BLOCKS
    block_owners = owners // BLOCKS

    def v_copy(dest, p):
        return pltpu.make_async_remote_copy(
            src_ref=v_ref.at[dest * PARTS + p], dst_ref=got_ref.at[p, me],
            send_sem=v_send.at[p, dest], recv_sem=v_recv.at[p], device_id={"lat": dest},
        )

    def send_block(block, p):
        def one(k, carry):
            dest = block * block_owners + lax.rem(me + k, block_owners)

            @pl.when(dest != me)
            def _():
                v_copy(dest, p).start()

            return carry

        lax.fori_loop(0, block_owners, one, 0)

    mid = n // 2
    lower = me < mid

    def order(k):
        low_half = lower == (k >= mid)
        return jnp.where(low_half, 0, mid) + lax.rem(me + k, mid)

    loads[4].wait()
    for step in range(BLOCKS):
        block = jnp.where(lower, BLOCKS - 1 - step, step)
        base = block * block_rows
        position = (iota((block_rows, 128), 0) + base).astype(F32)

        def deposit(i):
            cells = cells_ref[i]
            hot = jnp.concatenate(
                [
                    jnp.where(position == cells[q : q + 1, :], 1.0, 0.0).astype(BF16)
                    for q in range(QUADS)
                ],
                axis=1,
            )
            return dot(hot, rhs_ref[i])

        inno_ref[...] = deposit(0)

        def more(i, carry):
            inno_ref[...] += deposit(i)
            return carry

        lax.fori_loop(1, depth, more, 0)
        innovation = inno_ref[:, 0:128] + inno_ref[:, 128:256]
        field = perturb_ref[0, pl.ds(pl.multiple_of(base, 16), block_rows), :].astype(F32)
        high, low = split(field * innovation)
        vertical = dot(jnp.concatenate([high, low], axis=1), vert_both) + dot(high, vert_lo)
        v_ref[pl.ds(block * (block_rows // part_rows), block_rows // part_rows)] = (
            vertical.reshape(block_rows // part_rows, part_rows, columns)
        )
        send_block(block, 0)
    for p in range(1, PARTS):


        def send_part(k, carry):
            dest = order(k)

            @pl.when((dest != me) & (dest < owners))
            def _():
                v_copy(dest, p).start()

            return carry

        lax.fori_loop(0, n, send_part, 0)

    @pl.when(me < owners)
    def _():
        for p in range(PARTS):
            got_ref[p, me] = v_ref[me * PARTS + p]

    for p in range(1, PARTS):
        zonal_kernel(p)

    weights = [float(np.exp(np.float32(-0.5) * np.float32(d / 8.0) ** 2)) for d in range(n)]

    def m_copy(k, p):
        dest = order(k)
        return pltpu.make_async_remote_copy(
            src_ref=m_ref.at[p, dest], dst_ref=back_ref.at[p, me],
            send_sem=m_send.at[p, k], recv_sem=m_recv.at[p], device_id={"lat": dest},
        )

    @pl.when(me < owners)
    def _():
        for p in range(PARTS):
            arrived = got_ref.at[p, pl.ds(0, n - 1)]
            pltpu.make_async_copy(arrived, arrived, v_recv.at[p]).wait()

            def smooth(i, carry):
                rows = pl.ds(pl.multiple_of(i * 8, 8), 8)
                fields = [got_ref[p, r, rows, :] for r in range(n)]
                for r in range(n):
                    terms = [weights[abs(r - s)] * fields[s] for s in range(n)]
                    while len(terms) > 1:
                        terms = [terms[j] + terms[j + 1] for j in range(0, len(terms), 2)]
                    m_ref[p, r, rows, :] = terms[0]
                return carry

            lax.fori_loop(0, part_rows // 8, smooth, 0)

            def start_m(k, carry):
                m_copy(k, p).start()
                return carry

            lax.fori_loop(0, mid, start_m, 0)
            lax.fori_loop(mid + 1, n, start_m, 0)
            back_ref[p, me] = m_ref[p, me]

    def out_copy(step):
        rows = pl.ds(step * block_rows, block_rows)
        return pltpu.make_async_copy(sum_ref.at[rows], out_ref.at[0, rows], out_sem.at[step])

    for p in range(PARTS):
        for own, total in ((True, owners - 1), (False, owners)):

            @pl.when((me < owners) == own)
            def _():
                arrived = back_ref.at[p, pl.ds(0, total)]
                pltpu.make_async_copy(arrived, arrived, m_recv.at[p]).wait()

        both = jnp.concatenate(split(back_ref[p].reshape(half, columns)), axis=1)
        both_ref[p, 0:half, :] = both
        both_ref[p, half : 2 * half, :] = both
        for step in range(BLOCKS):
            rows = pl.ds(step * block_rows, block_rows)
            turn = pl.ds(step * (half // BLOCKS), half)
            wide = dot(g_hi[p], both_ref[p, turn, :])
            narrow = dot(g_lo[p], both_ref[p, turn, 0:128])
            total = wide[:, 0:128] + (wide[:, 128:256] + narrow)
            sum_ref[rows, :] = total if p == 0 else sum_ref[rows, :] + total
            if p == PARTS - 1:
                out_copy(step).start()

    def end_obs(k, carry):
        obs_copy(k).wait_send()
        return carry

    lax.fori_loop(1, n, end_obs, 0)
    for step in range(BLOCKS):
        out_copy(step).wait()
    for p in range(PARTS):

        def end_v(dest, carry):
            @pl.when(dest != me)
            def _():
                v_copy(dest, p).wait_send()

            return carry

        lax.fori_loop(0, owners, end_v, 0)

    @pl.when(me < owners)
    def _():
        for p in range(PARTS):

            def end_m(k, carry):
                m_copy(k, p).wait_send()
                return carry

            lax.fori_loop(0, mid, end_m, 0)
            lax.fori_loop(mid + 1, n, end_m, 0)


def local(n, mems, obs_rows, obs_band, obs_cell, obs_top, perturb, control):
    _, lon, columns = perturb.shape
    count, levels = obs_rows.shape
    chunk = -(-lon // (n * 8 * PARTS)) * 8 * PARTS
    owners, part_rows = lon // chunk, chunk // PARTS
    assert owners * chunk == lon and owners % BLOCKS == 0 and owners <= n
    half = owners * part_rows
    depth = mems * n // 16
    dma = pltpu.SemaphoreType.DMA
    zonal = pl.pallas_call(
        functools.partial(body, n, mems, owners, part_rows),
        out_shape=jax.ShapeDtypeStruct((1, lon, columns), F32),
        in_specs=[pl.BlockSpec(memory_space=pltpu.HBM)] * 5,
        out_specs=pl.BlockSpec(memory_space=pltpu.HBM),
        scratch_shapes=[
            pltpu.VMEM((levels, count), F32),
            pltpu.VMEM((1, count), jnp.int32),
            pltpu.VMEM((1, count), jnp.int32),
            pltpu.VMEM((1, count), jnp.int32),
            pltpu.VMEM((1, lon, columns), BF16),
            pltpu.SemaphoreType.DMA((5,)),
            pltpu.VMEM((n, 16, 128), F32),
            pltpu.VMEM((mems, n, 16, 128), F32),
            pltpu.VMEM((depth, 128 * QUADS, 256), BF16),
            pltpu.VMEM((depth, 8, 128), F32),
            pltpu.VMEM((lon // BLOCKS, 256), F32),
            pltpu.VMEM((owners * PARTS, part_rows, columns), F32),
            pltpu.VMEM((PARTS, n, part_rows, columns), F32),
            pltpu.VMEM((PARTS, n, part_rows, columns), F32),
            pltpu.VMEM((PARTS, owners, part_rows, columns), F32),
            pltpu.VMEM((PARTS, lon // BLOCKS, half), BF16),
            pltpu.VMEM((PARTS, lon // BLOCKS, half), BF16),
            pltpu.VMEM((PARTS, 2 * half, 256), BF16),
            pltpu.VMEM((lon, columns), F32),
            pltpu.SemaphoreType.DMA((BLOCKS,)),
            dma((n,)), dma(()), dma((mems,)), dma((mems,)),
            dma((PARTS, n)), dma((PARTS,)), dma((PARTS, n)), dma((PARTS,)),
        ],
        compiler_params=pltpu.CompilerParams(
            collective_id=0, has_side_effects=True, vmem_limit_bytes=56 * 1024 * 1024
        ),
    )(
        obs_rows.T, obs_band.reshape(1, count), obs_cell.reshape(1, count),
        obs_top.reshape(1, count), perturb,
    )
    return control.astype(F32) + zonal


def solution(mesh):
    return jax.shard_map(
        functools.partial(local, mesh.shape["lat"], mesh.shape["mem"]),
        mesh=mesh,
        in_specs=(
            P(("lat", "mem"), None),
            P(("lat", "mem"), None),
            P(("lat", "mem")),
            P(("lat", "mem")),
            P("lat", None, "mem"),
            P("lat", None, "mem"),
        ),
        out_specs=P("lat", None, "mem"),
        check_vma=False,
    )
```
